32 devices in a mesh: dp: 8 (over y, x, core), seq: 4 (over z).
Axes of the slice: x: 2, y: 2, z: 4, core: 2. Of those that a mesh axis runs over, the one named last changes fastest.
Arguments:
- inputs: bfloat16 [16, 2048, 640], P('dp', 'seq'), may hold values from -6 to 6
- cotangent: bfloat16 [16, 2048, 640], P('dp', 'seq'), may hold values from -6 to 6
- w_query: bfloat16 [640, 1024], P('seq', 'dp'), may hold values from -0.25 to 0.25
- w_key: bfloat16 [640, 256], P('seq', 'dp'), may hold values from -0.25 to 0.25
- w_value: bfloat16 [640, 256], P('seq', 'dp'), may hold values from -0.25 to 0.25
- w_out: bfloat16 [1024, 640], P('seq', 'dp'), may hold values from -0.1875 to 0.1875
- w_gate: bfloat16 [640, 2048], P('seq', 'dp'), may hold values from -0.25 to 0.25
- w_up: bfloat16 [640, 2048], P('seq', 'dp'), may hold values from -0.25 to 0.25
- w_down: bfloat16 [2048, 640], P('seq', 'dp'), may hold values from -0.125 to 0.125
- gains: bfloat16 [48, 64], P('seq', 'dp'), may hold values from -0.5 to 0.5
Outputs:
- outputs: bfloat16 [16, 2048, 640], P('dp', 'seq')
- grad_inputs: bfloat16 [16, 2048, 640], P('dp', 'seq')
- grad_query: float32 [640, 1024], P('seq', 'dp')
- grad_key: float32 [640, 256], P('seq', 'dp')
- grad_value: float32 [640, 256], P('seq', 'dp')
- grad_out: float32 [1024, 640], P('seq', 'dp')
- grad_gate: float32 [640, 2048], P('seq', 'dp')
- grad_up: float32 [640, 2048], P('seq', 'dp')
- grad_down: float32 [2048, 640], P('seq', 'dp')
- grad_gains: float32 [48, 64], P('seq', 'dp')
The draws below stay inside these ranges and needn't reach their ends.
All inputs are finite; a program needn't handle non-finite values.
Results may differ from the reference program's by a relative error of at most 0.022.
Values may be sent and summed in bfloat16 or wider, within the bound.
A program may use at most 192 MiB of HBM per device.

```python
import jax
import jax.numpy as jnp
from jax import lax

D = 640
HEADS = 4
HD = 256
FF = 2048
WINDOW = 512
GAIN_COLS = 64
SEQ_LEN = 2048
SEQS = 16
GAIN_ROWS = 48


def levels(key, shape, cuts, low, high):
    level, own = 1.0, jax.random.fold_in(key, 6)
    for axis_at, blocks in cuts:
        heights = jnp.exp(jax.random.uniform(jax.random.fold_in(own, axis_at), (blocks,), jnp.float32, low / len(cuts), high / len(cuts)))
        level = level * jnp.repeat(heights, shape[axis_at] // blocks).reshape([-1 if axis == axis_at else 1 for axis in range(len(shape))])
    return level


def gaussian(stream_key, extent, deviation, reach, shards=(), kind=jnp.bfloat16):
    array = jax.random.normal(stream_key, extent, jnp.float32) * deviation
    if len(shards) > 0:
        array = levels(stream_key, extent, shards, -0.22, 0.18) * array
    return jnp.clip(array, min=-reach, max=reach).astype(kind)


def setup_inputs(seed: int = 0) -> dict:
    seeds = jax.random.split(jax.random.key(seed), 11)
    inputs = gaussian(seeds[0], (SEQS, SEQ_LEN, D), 1.0, 6.0, ((0, 8), (1, 4)))
    cotangent = gaussian(seeds[1], (SEQS, SEQ_LEN, D), 1.0, 6.0, ((0, 8), (1, 4)))
    w_query = gaussian(seeds[2], (D, HEADS * HD), D ** -0.5, 0.25, ((0, 4), (1, 8)))
    w_key = gaussian(seeds[3], (D, HD), D ** -0.5, 0.25, ((0, 4), (1, 8)))
    w_value = gaussian(seeds[4], (D, HD), D ** -0.5, 0.25, ((0, 4), (1, 8)))
    w_out = gaussian(seeds[5], (HEADS * HD, D), (HEADS * HD) ** -0.5, 0.1875, ((0, 4), (1, 8)))
    w_gate = gaussian(seeds[6], (D, FF), D ** -0.5, 0.25, ((0, 4), (1, 8)))
    w_up = gaussian(seeds[7], (D, FF), D ** -0.5, 0.25, ((0, 4), (1, 8)))
    w_down = gaussian(seeds[8], (FF, D), FF ** -0.5, 0.125, ((0, 4), (1, 8)))
    gains = jnp.clip(jax.random.uniform(seeds[9], (GAIN_ROWS, GAIN_COLS), jnp.float32, -0.5, 0.5) * levels(seeds[9], (GAIN_ROWS, GAIN_COLS), ((0, 4), (1, 8)), -0.4, 0.0), -0.5, 0.5).astype(jnp.bfloat16)
    return dict(inputs=inputs, cotangent=cotangent, w_query=w_query, w_key=w_key, w_value=w_value, w_out=w_out, w_gate=w_gate, w_up=w_up, w_down=w_down, gains=gains)


@jax.custom_vjp
def low(v):
    return lax.optimization_barrier(v.astype(jnp.bfloat16)).astype(jnp.float32)

@jax.custom_vjp
def low_back(v):
    return v

def low_keep(v):
    return (low(v), None)

def low_pass(kept, grad):
    return (grad,)

def back_keep(v):
    return (v, None)

def back_low(kept, grad):
    return (low(grad),)
low.defvjp(low_keep, low_pass)
low_back.defvjp(back_keep, back_low)
HIGHEST = lax.Precision.HIGHEST
EPS = 1e-06
MASKED = -1e+30

def rms_norm(vector, scale_gain):
    factor = lax.rsqrt(lax.optimization_barrier(jnp.mean(vector * vector, axis=-1, keepdims=True)) + EPS)
    return vector * factor * (1.0 + scale_gain)

def angles(positions, head_width):
    ladder = jnp.arange(head_width // 2).astype(jnp.float32) * 2.0
    inverse = 10000.0 ** (-ladder / head_width)
    return positions[:, None] * inverse[None, :]

def rotate(vector, angle_table):
    middle_at = vector.shape[-1] // 2
    leading = vector[..., :middle_at]
    trailing = vector[..., middle_at:]
    cosine = jnp.cos(angle_table)
    sine_of = jnp.sin(angle_table)
    return jnp.concatenate([leading * cosine - trailing * sine_of, trailing * cosine + leading * sine_of], axis=-1)

def matmul(left_side, right_side):
    return jnp.einsum('...k,kn->...n', left_side, right_side, precision=HIGHEST)

def split_gains(gains):
    flat_gains = gains.reshape(-1)
    return (flat_gains[0:D], flat_gains[D:2 * D], flat_gains[2 * D:3 * D], flat_gains[3 * D:4 * D], flat_gains[4 * D:4 * D + HD], flat_gains[4 * D + HD:4 * D + 2 * HD])

def layer(inputs_f, w_query, w_key, w_value, w_out, w_gate, w_up, w_down, gains):
    g_attn_in, g_attn_out, g_ffw_in, g_ffw_out, g_query, g_key = split_gains(gains)
    group_count = inputs_f.shape[0]
    seq_length = inputs_f.shape[1]
    positions = jnp.arange(seq_length).astype(jnp.int32)
    angle_table = angles(positions.astype(jnp.float32), HD)
    normed = low(rms_norm(inputs_f, g_attn_in))
    q_lin = low_back(matmul(normed, w_query)).reshape(group_count, seq_length, HEADS, HD)
    k_lin = low_back(matmul(normed, w_key))
    v_lin = low_back(matmul(normed, w_value))
    queries = low(rotate(rms_norm(q_lin, g_query), angle_table[:, None, :]))
    keys_r = low(rotate(rms_norm(k_lin, g_key), angle_table))
    values_r = low(v_lin)
    scores = low_back(jnp.einsum('gqhd,gkd->ghqk', queries, keys_r, precision=HIGHEST) * HD ** (-0.5))
    distance = positions[:, None] - positions[None, :]
    allowed = (distance >= 0) & (distance < WINDOW)
    scores = jnp.where(allowed[None, None], scores, MASKED)
    attn_probs = low(jax.nn.softmax(scores, axis=-1))
    mixed_heads = low(low_back(jnp.einsum('ghqk,gkd->gqhd', attn_probs, values_r, precision=HIGHEST)))
    mixed_heads = mixed_heads.reshape(group_count, seq_length, HEADS * HD)
    attended = low_back(matmul(mixed_heads, w_out))
    middle = inputs_f + rms_norm(attended, g_attn_out)
    ffw_in = low(rms_norm(middle, g_ffw_in))
    gate_val = low_back(matmul(ffw_in, w_gate))
    up_val = low_back(matmul(ffw_in, w_up))
    hidden = low(jax.nn.gelu(gate_val, approximate=True) * up_val)
    down_val = low_back(matmul(hidden, w_down))
    return middle + rms_norm(down_val, g_ffw_out)

def reference(inputs, cotangent, w_query, w_key, w_value, w_out, w_gate, w_up, w_down, gains):
    params = tuple((weight_in.astype(jnp.float32) for weight_in in (w_query, w_key, w_value, w_out, w_gate, w_up, w_down, gains)))
    packed = 4
    shaped_in = inputs.astype(jnp.float32).reshape(SEQS // packed, packed, SEQ_LEN, D)
    shaped_cot = cotangent.astype(jnp.float32).reshape(SEQS // packed, packed, SEQ_LEN, D)

    def scan_step(running, pair_in):
        block_in, block_cot = pair_in
        result, pullback = jax.vjp(layer, block_in, *params)
        all_grads = pullback(block_cot)
        running = tuple((earlier + later for earlier, later in zip(running, all_grads[1:])))
        return (running, (result.astype(jnp.bfloat16), all_grads[0].astype(jnp.bfloat16)))
    zero_grads = tuple((jnp.zeros(weight_in.shape, jnp.float32) for weight_in in params))
    running, (result, grad_in) = lax.scan(scan_step, zero_grads, (shaped_in, shaped_cot))
    return (result.reshape(SEQS, SEQ_LEN, D), grad_in.reshape(SEQS, SEQ_LEN, D), running[0], running[1], running[2], running[3], running[4], running[5], running[6], running[7])
```

```python
import jax
import jax.numpy as jnp
from jax import lax
from jax.sharding import PartitionSpec as P

D = 640
HEADS = 4
HD = 256
WINDOW = 512
MB = 2


EPS = 1e-06
MASKED = -1e30


def shifted(value, axis, steps):
    count = lax.axis_size(axis)
    first, last = (max(0, -steps), min(count, count - steps))
    return lax.ppermute(value, axis, [(source, source + steps) for source in range(first, last)])


def rms_norm(vector, scale_gain):
    factor = lax.rsqrt(jnp.mean(vector * vector, axis=-1, keepdims=True) + EPS)
    return vector * factor * (1.0 + scale_gain)


def angles(positions, head_width):
    ladder = jnp.arange(head_width // 2).astype(jnp.float32) * 2.0
    inverse = 10000.0 ** (-ladder / head_width)
    return positions[:, None] * inverse[None, :]


def rotate(vector, angle_table):
    middle_at = vector.shape[-1] // 2
    leading = vector[..., :middle_at]
    trailing = vector[..., middle_at:]
    cosine = jnp.cos(angle_table)
    sine_of = jnp.sin(angle_table)
    return jnp.concatenate(
        [leading * cosine - trailing * sine_of, trailing * cosine + leading * sine_of], axis=-1
    )


def gated_unit(gate_val, up_val):
    return jax.nn.gelu(gate_val, approximate=True) * up_val


def product(left_side, right_side):
    flat_left = left_side.reshape(-1, left_side.shape[-1])
    result = jnp.dot(flat_left, right_side, preferred_element_type=jnp.float32)
    return result.reshape(left_side.shape[:-1] + (right_side.shape[-1],))


def outer_sum(left_side, right_side):
    flat_left = left_side.reshape(-1, left_side.shape[-1])
    flat_right = right_side.reshape(-1, right_side.shape[-1])
    return lax.dot_general(
        flat_left, flat_right, (((0,), (0,)), ((), ())), preferred_element_type=jnp.float32
    )


def back_product(gradient, weight):
    flat_grad = gradient.reshape(-1, gradient.shape[-1])
    result = lax.dot_general(
        flat_grad, weight, (((1,), (1,)), ((), ())), preferred_element_type=jnp.float32
    )
    return result.reshape(gradient.shape[:-1] + (weight.shape[0],))


def local_grads(function, primals, cotangent_in):
    return jax.vjp(function, *primals)[1](cotangent_in)


def split_gains(full_gains):
    flat_gains = full_gains.astype(jnp.float32).reshape(-1)
    return (
        flat_gains[0:D],
        flat_gains[D : 2 * D],
        flat_gains[2 * D : 3 * D],
        flat_gains[3 * D : 4 * D],
        flat_gains[4 * D : 4 * D + HD],
        flat_gains[4 * D + HD : 4 * D + 2 * HD],
    )


def masked_scores(queries, key_block, query_pos, key_pos):
    scores = jnp.einsum(
        "sqhd,skd->shqk", queries, key_block, preferred_element_type=jnp.float32
    ) * HD ** (-0.5)
    distance = query_pos[:, None] - key_pos[None, :]
    allowed = (distance >= 0) & (distance < WINDOW) & (key_pos[None, :] >= 0)
    return jnp.where(allowed[None, None], scores, MASKED)


def rms_back(vector, scale_gain, gradient):
    factor = lax.rsqrt(jnp.mean(vector * vector, axis=-1, keepdims=True) + EPS)
    scaled = vector * factor
    inner = gradient * (1.0 + scale_gain)
    d_vector = factor * (inner - scaled * jnp.mean(inner * scaled, axis=-1, keepdims=True))
    d_gain = jnp.sum(gradient * scaled, axis=tuple(range(vector.ndim - 1)))
    return d_vector, d_gain


def columns_joined(gathered):
    seqs, dps, rows, cols = gathered.shape
    return gathered.transpose(0, 2, 1, 3).reshape(seqs * rows, dps * cols)


def rows_joined(gathered):
    seqs, dps, rows, cols = gathered.shape
    return gathered.transpose(1, 2, 0, 3).reshape(dps * rows, seqs * cols)


def columns_parted(whole, seqs, dps):
    rows, cols = whole.shape
    return whole.reshape(seqs, rows // seqs, dps, cols // dps).transpose(2, 0, 1, 3)


def rows_parted(whole, seqs, dps):
    rows, cols = whole.shape
    return whole.reshape(dps, rows // dps, seqs, cols // seqs).transpose(0, 2, 1, 3)


def gather(packed):
    return lax.all_gather(packed, ("seq", "dp")).reshape(
        (lax.axis_size("seq"), lax.axis_size("dp")) + packed.shape
    )


def scatter(packed):
    return lax.psum_scatter(lax.psum_scatter(packed, "dp"), "seq")


def local(inputs, cotangent, w_query, w_key, w_value, w_out, w_gate, w_up, w_down, gains):
    groups, stretch_len = inputs.shape[:2]
    seqs, dps = lax.axis_size("seq"), lax.axis_size("dp")
    heads_width = HEADS * HD
    seq_index = lax.axis_index("seq")
    query_pos = seq_index * stretch_len + jnp.arange(stretch_len, dtype=jnp.int32)
    angle_table = angles(query_pos.astype(jnp.float32), HD)
    reach = WINDOW // stretch_len
    key_pos = (seq_index - reach) * stretch_len + jnp.arange(
        WINDOW + stretch_len, dtype=jnp.int32
    )
    rows_a, cols_q = w_query.shape
    cols_k = w_key.shape[1]
    rows_o = w_out.shape[1]
    rows_g, cols_g = gains.shape
    lead = cols_q + 2 * cols_k
    width = max(-(-(lead + cols_g) // 128) * 128, w_out.shape[0])

    def widened(value, rows, cols):
        return jnp.pad(value, ((0, rows - value.shape[0]), (0, cols - value.shape[1])))

    packed_one = jnp.concatenate(
        [
            widened(
                jnp.concatenate(
                    [w_query, w_key, w_value, widened(gains, rows_a, cols_g)], axis=1
                ),
                rows_a,
                width,
            ),
            widened(w_out.T, rows_o, width),
        ],
        axis=0,
    )
    cols_f = w_gate.shape[1]
    wide = max(2 * cols_f, w_down.shape[0])
    packed_two = jnp.concatenate(
        [
            widened(jnp.concatenate([w_gate, w_up], axis=1), rows_a, wide),
            widened(w_down.T, rows_o, wide),
        ],
        axis=0,
    )
    first = gather(packed_one)
    packed_two, first = lax.optimization_barrier((packed_two, first))
    second = gather(packed_two)

    full_query = columns_joined(first[:, :, :rows_a, :cols_q])
    full_key = columns_joined(first[:, :, :rows_a, cols_q : cols_q + cols_k])
    full_value = columns_joined(first[:, :, :rows_a, cols_q + cols_k : lead])
    full_gains = columns_joined(first[:, :, :rows_g, lead : lead + cols_g])
    out_t = rows_joined(first[:, :, rows_a:, : w_out.shape[0]])
    full_gate = columns_joined(second[:, :, :rows_a, :cols_f])
    full_up = columns_joined(second[:, :, :rows_a, cols_f : 2 * cols_f])
    down_t = rows_joined(second[:, :, rows_a:, : w_down.shape[0]])
    g_attn_in, g_attn_out, g_ffw_in, g_ffw_out, g_query, g_key = split_gains(full_gains)

    resid = inputs.astype(jnp.float32)
    normed = rms_norm(resid, g_attn_in).astype(jnp.bfloat16)
    q_lin = product(normed, full_query).reshape(groups, stretch_len, HEADS, HD)
    k_lin = product(normed, full_key)
    v_lin = product(normed, full_value)
    keys = rotate(rms_norm(k_lin, g_key), angle_table).astype(jnp.bfloat16)
    own = jnp.concatenate([keys, v_lin.astype(jnp.bfloat16)], axis=-1)
    parts = [own]
    for offset in range(1, reach + 1):
        parts.insert(0, shifted(own, "seq", offset))
    queries = rotate(rms_norm(q_lin, g_query), angle_table[:, None, :]).astype(jnp.bfloat16)
    block = jnp.concatenate(parts, axis=1)
    key_block, value_block = block[..., :HD], block[..., HD:]

    scores = masked_scores(queries, key_block, query_pos, key_pos)
    row_max = jnp.max(scores, axis=-1, keepdims=True)
    exponent = jnp.exp(scores - row_max)
    row_sum = jnp.sum(exponent, axis=-1, keepdims=True)
    probs = (exponent / row_sum).astype(jnp.bfloat16)
    log_sum = row_max + jnp.log(row_sum)
    mixed = jnp.einsum(
        "shqk,skd->sqhd", probs, value_block, preferred_element_type=jnp.float32
    )
    mixed = mixed.reshape(groups, stretch_len, heads_width).astype(jnp.bfloat16)

    attended = back_product(mixed, out_t)
    middle = resid + rms_norm(attended, g_attn_out)
    ffw_in = rms_norm(middle, g_ffw_in).astype(jnp.bfloat16)
    gate_val = product(ffw_in, full_gate)
    up_val = product(ffw_in, full_up)
    hidden = gated_unit(gate_val, up_val).astype(jnp.bfloat16)
    down_val = back_product(hidden, down_t)
    outputs = (middle + rms_norm(down_val, g_ffw_out)).astype(jnp.bfloat16)

    grad_out_f = cotangent.astype(jnp.float32)
    d_down, d_g_ffw_out = rms_back(down_val, g_ffw_out, grad_out_f)
    d_down = d_down.astype(jnp.bfloat16)
    d_hidden = product(d_down, down_t)
    d_gate, d_up = local_grads(gated_unit, (gate_val, up_val), d_hidden)
    d_gate = d_gate.astype(jnp.bfloat16)
    d_up = d_up.astype(jnp.bfloat16)
    d_ffw_in = back_product(d_gate, full_gate) + back_product(d_up, full_up)
    d_middle, d_g_ffw_in = rms_back(middle, g_ffw_in, d_ffw_in)
    d_middle = grad_out_f + d_middle
    d_attended, d_g_attn_out = rms_back(attended, g_attn_out, d_middle)
    d_attended = d_attended.astype(jnp.bfloat16)
    d_mixed = (
        product(d_attended, out_t)
        .astype(jnp.bfloat16)
        .reshape(groups, stretch_len, HEADS, HD)
    )
    low = jnp.bfloat16
    sum_gate = columns_parted(outer_sum(ffw_in, d_gate).astype(low), seqs, dps)
    sum_up = columns_parted(outer_sum(ffw_in, d_up).astype(low), seqs, dps)
    sum_down = rows_parted(outer_sum(d_down, hidden).astype(low), seqs, dps)
    def widened_four(value, rows, cols):
        return jnp.pad(
            value, ((0, 0), (0, 0), (0, rows - value.shape[2]), (0, cols - value.shape[3]))
        )

    early = scatter(
        jnp.concatenate(
            [
                widened_four(jnp.concatenate([sum_gate, sum_up], axis=3), rows_a, wide),
                widened_four(sum_down, rows_o, wide),
            ],
            axis=2,
        )
    )

    scores = masked_scores(queries, key_block, query_pos, key_pos)
    full_probs = jnp.exp(scores - log_sum)
    d_probs = jnp.einsum(
        "sqhd,skd->shqk", d_mixed, value_block, preferred_element_type=jnp.float32
    )
    d_scores = full_probs * (d_probs - jnp.sum(full_probs * d_probs, axis=-1, keepdims=True))
    d_scores = d_scores.astype(jnp.bfloat16)
    d_value_block = jnp.einsum(
        "shqk,sqhd->skd",
        full_probs.astype(jnp.bfloat16),
        d_mixed,
        preferred_element_type=jnp.float32,
    )
    d_key_block = jnp.einsum(
        "shqk,sqhd->skd", d_scores, queries, preferred_element_type=jnp.float32
    ) * HD ** (-0.5)
    d_queries = jnp.einsum(
        "shqk,skd->sqhd", d_scores, key_block, preferred_element_type=jnp.float32
    ) * HD ** (-0.5)
    d_block = jnp.concatenate([d_key_block, d_value_block], axis=-1)
    d_own = d_block[:, reach * stretch_len :]
    for offset in range(1, reach + 1):
        at = (reach - offset) * stretch_len
        d_own = d_own + shifted(
            d_block[:, at : at + stretch_len].astype(low), "seq", -offset
        ).astype(jnp.float32)

    def unrotate(gradient, table):
        return rotate(gradient, -table)

    d_q_lin, d_g_query = rms_back(q_lin, g_query, unrotate(d_queries, angle_table[:, None, :]))
    d_k_lin, d_g_key = rms_back(k_lin, g_key, unrotate(d_own[..., :HD], angle_table))
    d_q_lin = d_q_lin.reshape(groups, stretch_len, heads_width).astype(low)
    d_k_lin = d_k_lin.astype(low)
    d_values = d_own[..., HD:].astype(low)
    sum_query = columns_parted(outer_sum(normed, d_q_lin).astype(low), seqs, dps)
    sum_key = columns_parted(outer_sum(normed, d_k_lin).astype(low), seqs, dps)
    sum_value = columns_parted(outer_sum(normed, d_values).astype(low), seqs, dps)
    sum_out = rows_parted(outer_sum(d_attended, mixed).astype(low), seqs, dps)
    d_normed = (
        back_product(d_q_lin, full_query)
        + back_product(d_k_lin, full_key)
        + back_product(d_values, full_value)
    )
    d_resid, d_g_attn_in = rms_back(resid, g_attn_in, d_normed)
    grad_inputs = (d_middle + d_resid).astype(jnp.bfloat16)
    sum_gains = jnp.concatenate(
        [d_g_attn_in, d_g_attn_out, d_g_ffw_in, d_g_ffw_out, d_g_query, d_g_key]
    ).reshape(full_gains.shape)
    sum_gains = columns_parted(sum_gains.astype(low), seqs, dps)

    late = scatter(
        jnp.concatenate(
            [
                widened_four(
                    jnp.concatenate(
                        [sum_query, sum_key, sum_value, widened_four(sum_gains, rows_a, cols_g)],
                        axis=3,
                    ),
                    rows_a,
                    width,
                ),
                widened_four(sum_out, rows_o, width),
            ],
            axis=2,
        )
    )
    early = early.astype(jnp.float32)
    late = late.astype(jnp.float32)
    return (
        outputs,
        grad_inputs,
        late[:rows_a, :cols_q],
        late[:rows_a, cols_q : cols_q + cols_k],
        late[:rows_a, cols_q + cols_k : lead],
        late[rows_a:, : w_out.shape[0]].T,
        early[:rows_a, :cols_f],
        early[:rows_a, cols_f : 2 * cols_f],
        early[rows_a:, : w_down.shape[0]].T,
        late[:rows_g, lead : lead + cols_g],
    )


def solution(mesh):
    in_specs = (
        P("dp", "seq", None),
        P("dp", "seq", None),
        P("seq", "dp"),
        P("seq", "dp"),
        P("seq", "dp"),
        P("seq", "dp"),
        P("seq", "dp"),
        P("seq", "dp"),
        P("seq", "dp"),
        P("seq", "dp"),
    )
    out_specs = (
        P("dp", "seq", None),
        P("dp", "seq", None),
        P("seq", "dp"),
        P("seq", "dp"),
        P("seq", "dp"),
        P("seq", "dp"),
        P("seq", "dp"),
        P("seq", "dp"),
        P("seq", "dp"),
        P("seq", "dp"),
    )
    return jax.shard_map(local, mesh=mesh, in_specs=in_specs, out_specs=out_specs, check_vma=False)
```

```python
import functools
import math

import jax
import jax.numpy as jnp
from jax import lax
from jax.experimental import pallas as pl
from jax.experimental.pallas import tpu as pltpu
from jax.sharding import PartitionSpec as P

D = 640
HEADS = 4
HD = 256
WINDOW = 512
MB = 2


EPS = 1e-06
MASKED = -1e30


def shifted(value, axis, steps):
    count = lax.axis_size(axis)
    first, last = (max(0, -steps), min(count, count - steps))
    return lax.ppermute(value, axis, [(source, source + steps) for source in range(first, last)])


def rms_norm(vector, scale_gain):
    factor = lax.rsqrt(jnp.mean(vector * vector, axis=-1, keepdims=True) + EPS)
    return vector * factor * (1.0 + scale_gain)


def angles(positions, head_width):
    ladder = jnp.arange(head_width // 2).astype(jnp.float32) * 2.0
    inverse = 10000.0 ** (-ladder / head_width)
    return positions[:, None] * inverse[None, :]


def rotate(vector, angle_table):
    middle_at = vector.shape[-1] // 2
    leading = vector[..., :middle_at]
    trailing = vector[..., middle_at:]
    cosine = jnp.cos(angle_table)
    sine_of = jnp.sin(angle_table)
    return jnp.concatenate(
        [leading * cosine - trailing * sine_of, trailing * cosine + leading * sine_of], axis=-1
    )


def product(left_side, right_side):
    flat_left = left_side.reshape(-1, left_side.shape[-1])
    result = jnp.dot(flat_left, right_side, preferred_element_type=jnp.float32)
    return result.reshape(left_side.shape[:-1] + (right_side.shape[-1],))


def outer_sum(left_side, right_side):
    flat_left = left_side.reshape(-1, left_side.shape[-1])
    flat_right = right_side.reshape(-1, right_side.shape[-1])
    return lax.dot_general(
        flat_left, flat_right, (((0,), (0,)), ((), ())), preferred_element_type=jnp.float32
    )


def back_product(gradient, weight):
    flat_grad = gradient.reshape(-1, gradient.shape[-1])
    result = lax.dot_general(
        flat_grad, weight, (((1,), (1,)), ((), ())), preferred_element_type=jnp.float32
    )
    return result.reshape(gradient.shape[:-1] + (weight.shape[0],))


def split_gains(full_gains):
    flat_gains = full_gains.astype(jnp.float32).reshape(-1)
    return (
        flat_gains[0:D],
        flat_gains[D : 2 * D],
        flat_gains[2 * D : 3 * D],
        flat_gains[3 * D : 4 * D],
        flat_gains[4 * D : 4 * D + HD],
        flat_gains[4 * D + HD : 4 * D + 2 * HD],
    )


NN = (((1,), (0,)), ((), ()))
NT = (((1,), (1,)), ((), ()))
TN = (((0,), (0,)), ((), ()))
VMEM_BYTES = 60 * 2**20


def dot(left_side, right_side, dims):
    return lax.dot_general(left_side, right_side, dims, preferred_element_type=jnp.float32)


def heads_stacked(ref, rows):
    return jnp.concatenate([ref[0, rows, h * HD : (h + 1) * HD] for h in range(HEADS)], axis=0)


def exponentials(base, queries, keys, first):
    rows, span = queries.shape[0], keys.shape[0]
    scores = dot(queries, keys, NT) * HD ** (-0.5)
    row_at = lax.broadcasted_iota(jnp.int32, (rows, span), 0) % (rows // HEADS)
    key_at = lax.broadcasted_iota(jnp.int32, (rows, span), 1)
    distance = row_at + WINDOW - key_at
    allowed = (distance >= 0) & (distance < WINDOW) & (base + first + key_at >= 0)
    return jnp.where(allowed, jnp.exp(scores), 0.0)


def attend_kernel(step, base_ref, q_ref, kv_ref, mixed_ref):
    length = q_ref.shape[1]
    for first in range(0, length, step):
        rows, span = pl.ds(first, step), pl.ds(first, step + WINDOW)
        queries = heads_stacked(q_ref, rows)
        exponent = exponentials(base_ref[0], queries, kv_ref[0, span, :HD], first)
        row_sum = jnp.sum(exponent, axis=-1, keepdims=True)
        mixed = dot(exponent.astype(jnp.bfloat16), kv_ref[0, span, HD:], NN) / row_sum
        for h in range(HEADS):
            mixed_ref[0, rows, h * HD : (h + 1) * HD] = mixed[
                h * step : (h + 1) * step
            ].astype(jnp.bfloat16)


def attend(base, queries, block):
    groups, length, wide = queries.shape
    span = block.shape[1]
    step = min(256, length)
    return pl.pallas_call(
        functools.partial(attend_kernel, step),
        grid=(groups,),
        in_specs=[
            pl.BlockSpec(memory_space=pltpu.SMEM),
            pl.BlockSpec((1, length, wide), lambda g: (g, 0, 0)),
            pl.BlockSpec((1, span, 2 * HD), lambda g: (g, 0, 0)),
        ],
        out_specs=pl.BlockSpec((1, length, wide), lambda g: (g, 0, 0)),
        out_shape=jax.ShapeDtypeStruct(queries.shape, jnp.bfloat16),
        compiler_params=pltpu.CompilerParams(vmem_limit_bytes=VMEM_BYTES),
        cost_estimate=pl.CostEstimate(
            flops=4 * groups * length * wide * span, bytes_accessed=8 * 2**20, transcendentals=0
        ),
    )(base, queries, block)


def attend_back_kernel(step, base_ref, q_ref, kv_ref, d_mixed_ref, d_q_ref, d_kv_ref):
    length = q_ref.shape[1]
    d_kv_ref[...] = jnp.zeros_like(d_kv_ref)
    for first in range(0, length, step):
        rows, span = pl.ds(first, step), pl.ds(first, step + WINDOW)
        queries = heads_stacked(q_ref, rows)
        d_mixed = heads_stacked(d_mixed_ref, rows)
        keys, values = kv_ref[0, span, :HD], kv_ref[0, span, HD:]
        exponent = exponentials(base_ref[0], queries, keys, first)
        probs = exponent * (1.0 / jnp.sum(exponent, axis=-1, keepdims=True))
        d_probs = dot(d_mixed, values, NT)
        inner = jnp.sum(probs * d_probs, axis=-1, keepdims=True)
        d_scores = (probs * (d_probs - inner)).astype(jnp.bfloat16)
        d_kv_ref[0, span, HD:] += dot(probs.astype(jnp.bfloat16), d_mixed, TN)
        d_kv_ref[0, span, :HD] += dot(d_scores, queries, TN) * HD ** (-0.5)
        d_queries = dot(d_scores, keys, NN) * HD ** (-0.5)
        for h in range(HEADS):
            d_q_ref[0, rows, h * HD : (h + 1) * HD] = d_queries[h * step : (h + 1) * step]


def attend_back(base, queries, block, d_mixed):
    groups, length, wide = queries.shape
    span = block.shape[1]
    step = min(256, length)
    whole = pl.BlockSpec((1, length, wide), lambda g: (g, 0, 0))
    ahead = pl.BlockSpec((1, span, 2 * HD), lambda g: (g, 0, 0))
    return pl.pallas_call(
        functools.partial(attend_back_kernel, step),
        grid=(groups,),
        in_specs=[pl.BlockSpec(memory_space=pltpu.SMEM), whole, ahead, whole],
        out_specs=[whole, ahead],
        out_shape=[
            jax.ShapeDtypeStruct(queries.shape, jnp.float32),
            jax.ShapeDtypeStruct(block.shape, jnp.float32),
        ],
        compiler_params=pltpu.CompilerParams(vmem_limit_bytes=VMEM_BYTES),
        cost_estimate=pl.CostEstimate(
            flops=10 * groups * length * wide * span, bytes_accessed=16 * 2**20, transcendentals=0
        ),
    )(base, queries, block, d_mixed)


def normed_back(vector, factor, plus_gain, gradient):
    scaled = vector * factor
    inner = gradient * plus_gain
    d_vector = factor * (inner - scaled * jnp.mean(inner * scaled, axis=-1, keepdims=True))
    return d_vector, jnp.sum(gradient * scaled, axis=0, keepdims=True)


def factor_of(vector):
    return lax.rsqrt(jnp.mean(vector * vector, axis=-1, keepdims=True) + EPS)


def middle_kernel(
    sizes, x_ref, cot_ref, mixed_ref, gains_ref, *refs
):
    if sizes is None:
        out_t, gate, up, down_t = refs[:4]
        outs = refs[4:]
    else:
        first, second = refs[:2]
        outs = refs[2:12]
        out_t, gate, up, down_t = refs[12:]
    (
        y_ref, d_middle_ref, d_mixed_ref, hidden_ref, d_gate_ref, d_up_ref, ffw_in_ref,
        d_down_ref, d_attended_ref, d_gains_ref,
    ) = outs
    low = jnp.bfloat16

    @pl.when(pl.program_id(0) == 0)
    def _():
        d_gains_ref[...] = jnp.zeros_like(d_gains_ref)
        if sizes is not None:
            rows_a, rows_o, cols_f, cols_o, cols_d = sizes
            for s in range(first.shape[0]):
                for d in range(first.shape[1]):
                    tall, flat = pl.ds(s * rows_a, rows_a), pl.ds(d * rows_o, rows_o)
                    wide = pl.ds(d * cols_f, cols_f)
                    gate[tall, wide] = second[s, d, :rows_a, :cols_f]
                    up[tall, wide] = second[s, d, :rows_a, cols_f : 2 * cols_f]
                    down_t[flat, pl.ds(s * cols_d, cols_d)] = second[s, d, rows_a:, :cols_d]
                    out_t[flat, pl.ds(s * cols_o, cols_o)] = first[s, d, :, :cols_o]

    x, grad = x_ref[...].astype(jnp.float32), cot_ref[...].astype(jnp.float32)
    plus = [1.0 + gains_ref[r : r + 1, :] for r in range(4)]
    attended = dot(mixed_ref[...], out_t[...], NT)
    attended_factor = factor_of(attended)
    middle = x + attended * attended_factor * plus[1]
    middle_factor = factor_of(middle)
    ffw_in = (middle * middle_factor * plus[2]).astype(low)
    ffw_in_ref[...] = ffw_in
    a = dot(ffw_in, gate[...], NN)
    b = dot(ffw_in, up[...], NN)
    slope = math.sqrt(2.0 / math.pi)
    square = a * a
    bend = jnp.tanh(slope * a * (1.0 + 0.044715 * square))
    half = 0.5 * (1.0 + bend)
    gelu = a * half
    hidden = (gelu * b).astype(low)
    hidden_ref[...] = hidden
    down = dot(hidden, down_t[...], NT)
    down_factor = factor_of(down)
    y_ref[...] = (middle + down * down_factor * plus[3]).astype(low)
    d_down, d_out_gain = normed_back(down, down_factor, plus[3], grad)
    d_down = d_down.astype(low)
    d_down_ref[...] = d_down
    d_hidden = dot(d_down, down_t[...], NN)
    d_up = (d_hidden * gelu).astype(low)
    d_up_ref[...] = d_up
    gelu_slope = half + 0.5 * a * (1.0 - bend * bend) * (
        slope * (1.0 + 3.0 * 0.044715 * square)
    )
    d_gate = (d_hidden * b * gelu_slope).astype(low)
    d_gate_ref[...] = d_gate
    d_ffw_in = dot(d_gate, gate[...], NT) + dot(d_up, up[...], NT)
    d_middle, d_in_gain = normed_back(middle, middle_factor, plus[2], d_ffw_in)
    d_middle = grad + d_middle
    d_middle_ref[...] = d_middle
    d_attended, d_attn_gain = normed_back(attended, attended_factor, plus[1], d_middle)
    d_attended = d_attended.astype(low)
    d_attended_ref[...] = d_attended
    d_mixed_ref[...] = dot(d_attended, out_t[...], NN).astype(low)
    d_gains_ref[1:2, :] += d_attn_gain
    d_gains_ref[2:3, :] += d_in_gain
    d_gains_ref[3:4, :] += d_out_gain


def middle_part(x, cot, mixed, gains_four, weights, sizes, ff):
    tokens = x.shape[0]
    step = min(256, tokens)
    low = jnp.bfloat16
    wide = mixed.shape[1]

    def rows(cols):
        return pl.BlockSpec((step, cols), lambda i: (i, 0))

    def fixed(shape):
        return pl.BlockSpec(
            shape, lambda i: (0,) * len(shape), pipeline_mode=pl.Buffered(1)
        )

    outs = [
        (D, low), (D, jnp.float32), (wide, low), (ff, low), (ff, low), (ff, low), (D, low),
        (D, low), (D, low),
    ]
    scratch = []
    if sizes is not None:
        scratch = [pltpu.VMEM((D, cols), low) for cols in (wide, ff, ff, ff)]
    return pl.pallas_call(
        functools.partial(middle_kernel, sizes),
        grid=(tokens // step,),
        in_specs=[rows(D), rows(D), rows(wide), fixed((8, D))]
        + [fixed(weight.shape) for weight in weights],
        out_specs=[rows(cols) for cols, _ in outs] + [pl.BlockSpec((8, D), lambda i: (0, 0))],
        out_shape=[jax.ShapeDtypeStruct((tokens, cols), kind) for cols, kind in outs]
        + [jax.ShapeDtypeStruct((8, D), jnp.float32)],
        scratch_shapes=scratch,
        compiler_params=pltpu.CompilerParams(vmem_limit_bytes=VMEM_BYTES),
        cost_estimate=pl.CostEstimate(
            flops=4 * tokens * D * (3 * ff + wide), bytes_accessed=40 * 2**20, transcendentals=0
        ),
    )(x, cot, mixed, gains_four, *weights)


def sums_kernel(seqs, rows_a, rows_o, cols_f, ffw_in, d_down, d_gate, d_up, hidden, out):
    at = pl.program_id(0)
    low = jnp.bfloat16
    each = d_gate.shape[1] // cols_f
    for half, gradient in enumerate((d_gate, d_up)):
        total = dot(ffw_in[...], gradient[...], TN).astype(low)
        for e in range(each):
            for s in range(seqs):
                out[at * each + e, s, :rows_a, half * cols_f : (half + 1) * cols_f] = total[
                    s * rows_a : (s + 1) * rows_a, e * cols_f : (e + 1) * cols_f
                ]
    total = dot(d_down[...], hidden[...], TN).astype(low)
    for d in range(out.shape[0]):
        out[d, at, rows_a:, :] = total[d * rows_o : (d + 1) * rows_o, :]


def packed_sums(seqs, dps, sizes, ffw_in, d_down, d_gate, d_up, hidden):
    rows_a, rows_o, cols_f, _, cols_d = sizes
    tokens = ffw_in.shape[0]
    shape = (dps, seqs, rows_a + rows_o, cols_d)
    whole = pl.BlockSpec((tokens, D), lambda i: (0, 0))
    part = pl.BlockSpec((tokens, cols_d), lambda i: (0, i))
    return pl.pallas_call(
        functools.partial(sums_kernel, seqs, rows_a, rows_o, cols_f),
        grid=(seqs,),
        in_specs=[whole, whole, part, part, part],
        out_specs=pl.BlockSpec(shape, lambda i: (0, 0, 0, 0)),
        out_shape=jax.ShapeDtypeStruct(shape, jnp.bfloat16),
        compiler_params=pltpu.CompilerParams(vmem_limit_bytes=VMEM_BYTES),
        cost_estimate=pl.CostEstimate(
            flops=6 * tokens * D * cols_d * seqs, bytes_accessed=24 * 2**20, transcendentals=0
        ),
    )(ffw_in, d_down, d_gate, d_up, hidden)


def rms_back(vector, scale_gain, gradient):
    factor = lax.rsqrt(jnp.mean(vector * vector, axis=-1, keepdims=True) + EPS)
    scaled = vector * factor
    inner = gradient * (1.0 + scale_gain)
    d_vector = factor * (inner - scaled * jnp.mean(inner * scaled, axis=-1, keepdims=True))
    d_gain = jnp.sum(gradient * scaled, axis=tuple(range(vector.ndim - 1)))
    return d_vector, d_gain


def columns_joined(gathered):
    seqs, dps, rows, cols = gathered.shape
    return gathered.transpose(0, 2, 1, 3).reshape(seqs * rows, dps * cols)


def rows_joined(gathered):
    seqs, dps, rows, cols = gathered.shape
    return gathered.transpose(1, 2, 0, 3).reshape(dps * rows, seqs * cols)


def columns_parted(whole, seqs, dps):
    rows, cols = whole.shape
    return whole.reshape(seqs, rows // seqs, dps, cols // dps).transpose(2, 0, 1, 3)


def rows_parted(whole, seqs, dps):
    rows, cols = whole.shape
    return whole.reshape(dps, rows // dps, seqs, cols // seqs).transpose(0, 2, 1, 3)


def gather(packed):
    return lax.all_gather(packed, ("seq", "dp")).reshape(
        (lax.axis_size("seq"), lax.axis_size("dp")) + packed.shape
    )


def scatter(packed):
    return lax.psum_scatter(lax.psum_scatter(packed, "dp"), "seq")


def local(inputs, cotangent, w_query, w_key, w_value, w_out, w_gate, w_up, w_down, gains):
    groups, stretch_len = inputs.shape[:2]
    seqs, dps = lax.axis_size("seq"), lax.axis_size("dp")
    heads_width = HEADS * HD
    seq_index = lax.axis_index("seq")
    query_pos = seq_index * stretch_len + jnp.arange(stretch_len, dtype=jnp.int32)
    angle_table = angles(query_pos.astype(jnp.float32), HD)
    reach = WINDOW // stretch_len
    rows_a, cols_q = w_query.shape
    cols_k = w_key.shape[1]
    rows_o = w_out.shape[1]
    rows_g, cols_g = gains.shape
    lead = cols_q + 2 * cols_k
    width = max(-(-(lead + cols_g) // 128) * 128, w_out.shape[0])

    def widened(value, rows, cols):
        return jnp.pad(value, ((0, rows - value.shape[0]), (0, cols - value.shape[1])))

    packed_one = jnp.concatenate(
        [
            widened(
                jnp.concatenate(
                    [w_query, w_key, w_value, widened(gains, rows_a, cols_g)], axis=1
                ),
                rows_a,
                width,
            ),
            widened(w_out.T, rows_o, width),
        ],
        axis=0,
    )
    cols_f = w_gate.shape[1]
    wide = max(2 * cols_f, w_down.shape[0])
    packed_two = jnp.concatenate(
        [
            widened(jnp.concatenate([w_gate, w_up], axis=1), rows_a, wide),
            widened(w_down.T, rows_o, wide),
        ],
        axis=0,
    )
    first = gather(packed_one)
    packed_two, first = lax.optimization_barrier((packed_two, first))
    second = gather(packed_two)

    full_query = columns_joined(first[:, :, :rows_a, :cols_q])
    full_key = columns_joined(first[:, :, :rows_a, cols_q : cols_q + cols_k])
    full_value = columns_joined(first[:, :, :rows_a, cols_q + cols_k : lead])
    full_gains = columns_joined(first[:, :, :rows_g, lead : lead + cols_g])
    cols_o, cols_d = w_out.shape[0], w_down.shape[0]
    sizes = (rows_a, rows_o, cols_f, cols_o, cols_d)
    aligned = (
        rows_a % 16 == 0
        and rows_o % 16 == 0
        and cols_f % 128 == 0
        and cols_o % 128 == 0
        and cols_d == 2 * cols_f
        and dps == 2 * seqs
    )
    if aligned:
        weights = (first[:, :, rows_a:, :], second)
    else:
        weights = (
            rows_joined(first[:, :, rows_a:, :cols_o]),
            columns_joined(second[:, :, :rows_a, :cols_f]),
            columns_joined(second[:, :, :rows_a, cols_f : 2 * cols_f]),
            rows_joined(second[:, :, rows_a:, :cols_d]),
        )
    g_attn_in, g_attn_out, g_ffw_in, g_ffw_out, g_query, g_key = split_gains(full_gains)

    resid = inputs.astype(jnp.float32)
    normed = rms_norm(resid, g_attn_in).astype(jnp.bfloat16)
    q_lin = product(normed, full_query).reshape(groups, stretch_len, HEADS, HD)
    k_lin = product(normed, full_key)
    v_lin = product(normed, full_value)
    keys = rotate(rms_norm(k_lin, g_key), angle_table).astype(jnp.bfloat16)
    own = jnp.concatenate([keys, v_lin.astype(jnp.bfloat16)], axis=-1)
    parts = [own]
    for offset in range(1, reach + 1):
        parts.insert(0, shifted(own, "seq", offset))
    queries = rotate(rms_norm(q_lin, g_query), angle_table[:, None, :]).astype(jnp.bfloat16)
    block = jnp.concatenate(parts, axis=1)

    base = ((seq_index - reach) * stretch_len).astype(jnp.int32).reshape(1)
    low = jnp.bfloat16
    tokens = groups * stretch_len
    queries = queries.reshape(groups, stretch_len, heads_width)
    mixed = attend(base, queries, block).reshape(tokens, heads_width)
    gains_four = jnp.pad(
        jnp.stack([g_attn_in, g_attn_out, g_ffw_in, g_ffw_out]), ((0, 4), (0, 0))
    )
    (
        outputs, d_middle, d_mixed, hidden, d_gate, d_up, ffw_in, d_down, d_attended, d_gains
    ) = middle_part(
        inputs.reshape(tokens, D),
        cotangent.reshape(tokens, D),
        mixed,
        gains_four,
        weights,
        sizes if aligned else None,
        cols_f * dps,
    )
    outputs = outputs.reshape(inputs.shape)
    d_middle = d_middle.reshape(inputs.shape)
    d_mixed = d_mixed.reshape(groups, stretch_len, heads_width)

    def widened_four(value, rows, cols):
        return jnp.pad(
            value, ((0, 0), (0, 0), (0, rows - value.shape[2]), (0, cols - value.shape[3]))
        )

    if aligned:
        early = packed_sums(seqs, dps, sizes, ffw_in, d_down, d_gate, d_up, hidden)
    else:
        sum_gate = columns_parted(outer_sum(ffw_in, d_gate).astype(low), seqs, dps)
        sum_up = columns_parted(outer_sum(ffw_in, d_up).astype(low), seqs, dps)
        sum_down = rows_parted(outer_sum(d_down, hidden).astype(low), seqs, dps)
        early = jnp.concatenate(
            [
                widened_four(jnp.concatenate([sum_gate, sum_up], axis=3), rows_a, wide),
                widened_four(sum_down, rows_o, wide),
            ],
            axis=2,
        )
    early, d_mixed = lax.optimization_barrier((early, d_mixed))
    early = scatter(early)

    d_queries, d_block = attend_back(base, queries, block, d_mixed)
    d_queries = d_queries.reshape(groups, stretch_len, HEADS, HD)
    d_own = d_block[:, reach * stretch_len :]
    for offset in range(1, reach + 1):
        at = (reach - offset) * stretch_len
        d_own = d_own + shifted(
            d_block[:, at : at + stretch_len].astype(low), "seq", -offset
        ).astype(jnp.float32)

    def unrotate(gradient, table):
        return rotate(gradient, -table)

    d_q_lin, d_g_query = rms_back(q_lin, g_query, unrotate(d_queries, angle_table[:, None, :]))
    d_k_lin, d_g_key = rms_back(k_lin, g_key, unrotate(d_own[..., :HD], angle_table))
    d_q_lin = d_q_lin.reshape(groups, stretch_len, heads_width).astype(low)
    d_k_lin = d_k_lin.astype(low)
    d_values = d_own[..., HD:].astype(low)
    sum_query = columns_parted(outer_sum(normed, d_q_lin).astype(low), seqs, dps)
    sum_key = columns_parted(outer_sum(normed, d_k_lin).astype(low), seqs, dps)
    sum_value = columns_parted(outer_sum(normed, d_values).astype(low), seqs, dps)
    sum_out = rows_parted(outer_sum(d_attended, mixed).astype(low), seqs, dps)
    d_normed = (
        back_product(d_q_lin, full_query)
        + back_product(d_k_lin, full_key)
        + back_product(d_values, full_value)
    )
    d_resid, d_g_attn_in = rms_back(resid, g_attn_in, d_normed)
    grad_inputs = (d_middle + d_resid).astype(jnp.bfloat16)
    sum_gains = jnp.concatenate(
        [d_g_attn_in, d_gains[1], d_gains[2], d_gains[3], d_g_query, d_g_key]
    ).reshape(full_gains.shape)
    sum_gains = columns_parted(sum_gains.astype(low), seqs, dps)

    late = scatter(
        jnp.concatenate(
            [
                widened_four(
                    jnp.concatenate(
                        [sum_query, sum_key, sum_value, widened_four(sum_gains, rows_a, cols_g)],
                        axis=3,
                    ),
                    rows_a,
                    width,
                ),
                widened_four(sum_out, rows_o, width),
            ],
            axis=2,
        )
    )
    early = early.astype(jnp.float32)
    late = late.astype(jnp.float32)
    return (
        outputs,
        grad_inputs,
        late[:rows_a, :cols_q],
        late[:rows_a, cols_q : cols_q + cols_k],
        late[:rows_a, cols_q + cols_k : lead],
        late[rows_a:, : w_out.shape[0]].T,
        early[:rows_a, :cols_f],
        early[:rows_a, cols_f : 2 * cols_f],
        early[rows_a:, : w_down.shape[0]].T,
        late[:rows_g, lead : lead + cols_g],
    )


def solution(mesh):
    in_specs = (
        P("dp", "seq", None),
        P("dp", "seq", None),
        P("seq", "dp"),
        P("seq", "dp"),
        P("seq", "dp"),
        P("seq", "dp"),
        P("seq", "dp"),
        P("seq", "dp"),
        P("seq", "dp"),
        P("seq", "dp"),
    )
    out_specs = (
        P("dp", "seq", None),
        P("dp", "seq", None),
        P("seq", "dp"),
        P("seq", "dp"),
        P("seq", "dp"),
        P("seq", "dp"),
        P("seq", "dp"),
        P("seq", "dp"),
        P("seq", "dp"),
        P("seq", "dp"),
    )
    return jax.shard_map(local, mesh=mesh, in_specs=in_specs, out_specs=out_specs, check_vma=False)
```

```python
import functools
import math

import jax
import jax.numpy as jnp
from jax import lax
from jax.experimental import pallas as pl
from jax.experimental.pallas import tpu as pltpu
from jax.sharding import PartitionSpec as P

D = 640
HEADS = 4
HD = 256
WINDOW = 512
MB = 2


EPS = 1e-06
MASKED = -1e30


def shifted(value, axis, steps):
    count = lax.axis_size(axis)
    first, last = (max(0, -steps), min(count, count - steps))
    return lax.ppermute(value, axis, [(source, source + steps) for source in range(first, last)])


def rms_norm(vector, scale_gain):
    factor = lax.rsqrt(jnp.mean(vector * vector, axis=-1, keepdims=True) + EPS)
    return vector * factor * (1.0 + scale_gain)


def angles(positions, head_width):
    ladder = jnp.arange(head_width // 2).astype(jnp.float32) * 2.0
    inverse = 10000.0 ** (-ladder / head_width)
    return positions[:, None] * inverse[None, :]


def rotate(vector, angle_table):
    middle_at = vector.shape[-1] // 2
    leading = vector[..., :middle_at]
    trailing = vector[..., middle_at:]
    cosine = jnp.cos(angle_table)
    sine_of = jnp.sin(angle_table)
    return jnp.concatenate(
        [leading * cosine - trailing * sine_of, trailing * cosine + leading * sine_of], axis=-1
    )


def product(left_side, right_side):
    flat_left = left_side.reshape(-1, left_side.shape[-1])
    result = jnp.dot(flat_left, right_side, preferred_element_type=jnp.float32)
    return result.reshape(left_side.shape[:-1] + (right_side.shape[-1],))


def outer_sum(left_side, right_side):
    flat_left = left_side.reshape(-1, left_side.shape[-1])
    flat_right = right_side.reshape(-1, right_side.shape[-1])
    return lax.dot_general(
        flat_left, flat_right, (((0,), (0,)), ((), ())), preferred_element_type=jnp.float32
    )


def back_product(gradient, weight):
    flat_grad = gradient.reshape(-1, gradient.shape[-1])
    result = lax.dot_general(
        flat_grad, weight, (((1,), (1,)), ((), ())), preferred_element_type=jnp.float32
    )
    return result.reshape(gradient.shape[:-1] + (weight.shape[0],))


def split_gains(full_gains):
    flat_gains = full_gains.astype(jnp.float32).reshape(-1)
    return (
        flat_gains[0:D],
        flat_gains[D : 2 * D],
        flat_gains[2 * D : 3 * D],
        flat_gains[3 * D : 4 * D],
        flat_gains[4 * D : 4 * D + HD],
        flat_gains[4 * D + HD : 4 * D + 2 * HD],
    )


NN = (((1,), (0,)), ((), ()))
NT = (((1,), (1,)), ((), ()))
TN = (((0,), (0,)), ((), ()))
VMEM_BYTES = 60 * 2**20


def dot(left_side, right_side, dims):
    return lax.dot_general(left_side, right_side, dims, preferred_element_type=jnp.float32)


def heads_stacked(ref, rows):
    return jnp.concatenate([ref[0, rows, h * HD : (h + 1) * HD] for h in range(HEADS)], axis=0)


def exponentials(base, queries, keys, first):
    rows, span = queries.shape[0], keys.shape[0]
    scores = dot(queries, keys, NT) * HD ** (-0.5)
    row_at = lax.broadcasted_iota(jnp.int32, (rows, span), 0) % (rows // HEADS)
    key_at = lax.broadcasted_iota(jnp.int32, (rows, span), 1)
    distance = row_at + WINDOW - key_at
    allowed = (distance >= 0) & (distance < WINDOW) & (base + first + key_at >= 0)
    return jnp.where(allowed, jnp.exp(scores), 0.0)


def attend_kernel(step, base_ref, q_ref, kv_ref, mixed_ref):
    length = q_ref.shape[1]
    for first in range(0, length, step):
        rows, span = pl.ds(first, step), pl.ds(first, step + WINDOW)
        queries = heads_stacked(q_ref, rows)
        exponent = exponentials(base_ref[0], queries, kv_ref[0, span, :HD], first)
        row_sum = jnp.sum(exponent, axis=-1, keepdims=True)
        mixed = dot(exponent.astype(jnp.bfloat16), kv_ref[0, span, HD:], NN) / row_sum
        for h in range(HEADS):
            mixed_ref[0, rows, h * HD : (h + 1) * HD] = mixed[
                h * step : (h + 1) * step
            ].astype(jnp.bfloat16)


def attend(base, queries, block):
    groups, length, wide = queries.shape
    span = block.shape[1]
    step = min(256, length)
    return pl.pallas_call(
        functools.partial(attend_kernel, step),
        grid=(groups,),
        in_specs=[
            pl.BlockSpec(memory_space=pltpu.SMEM),
            pl.BlockSpec((1, length, wide), lambda g: (g, 0, 0)),
            pl.BlockSpec((1, span, 2 * HD), lambda g: (g, 0, 0)),
        ],
        out_specs=pl.BlockSpec((1, length, wide), lambda g: (g, 0, 0)),
        out_shape=jax.ShapeDtypeStruct(queries.shape, jnp.bfloat16),
        compiler_params=pltpu.CompilerParams(vmem_limit_bytes=VMEM_BYTES),
        cost_estimate=pl.CostEstimate(
            flops=4 * groups * length * wide * span, bytes_accessed=8 * 2**20, transcendentals=0
        ),
    )(base, queries, block)


def attend_back_kernel(step, base_ref, q_ref, kv_ref, d_mixed_ref, d_q_ref, d_kv_ref):
    length = q_ref.shape[1]
    d_kv_ref[...] = jnp.zeros_like(d_kv_ref)
    for first in range(0, length, step):
        rows, span = pl.ds(first, step), pl.ds(first, step + WINDOW)
        queries = heads_stacked(q_ref, rows)
        d_mixed = heads_stacked(d_mixed_ref, rows)
        keys, values = kv_ref[0, span, :HD], kv_ref[0, span, HD:]
        exponent = exponentials(base_ref[0], queries, keys, first)
        probs = exponent * (1.0 / jnp.sum(exponent, axis=-1, keepdims=True))
        d_probs = dot(d_mixed, values, NT)
        inner = jnp.sum(probs * d_probs, axis=-1, keepdims=True)
        d_scores = (probs * (d_probs - inner)).astype(jnp.bfloat16)
        d_kv_ref[0, span, HD:] += dot(probs.astype(jnp.bfloat16), d_mixed, TN)
        d_kv_ref[0, span, :HD] += dot(d_scores, queries, TN) * HD ** (-0.5)
        d_queries = dot(d_scores, keys, NN) * HD ** (-0.5)
        for h in range(HEADS):
            d_q_ref[0, rows, h * HD : (h + 1) * HD] = d_queries[h * step : (h + 1) * step]


def attend_back(base, queries, block, d_mixed):
    groups, length, wide = queries.shape
    span = block.shape[1]
    step = min(256, length)
    whole = pl.BlockSpec((1, length, wide), lambda g: (g, 0, 0))
    ahead = pl.BlockSpec((1, span, 2 * HD), lambda g: (g, 0, 0))
    return pl.pallas_call(
        functools.partial(attend_back_kernel, step),
        grid=(groups,),
        in_specs=[pl.BlockSpec(memory_space=pltpu.SMEM), whole, ahead, whole],
        out_specs=[whole, ahead],
        out_shape=[
            jax.ShapeDtypeStruct(queries.shape, jnp.float32),
            jax.ShapeDtypeStruct(block.shape, jnp.float32),
        ],
        compiler_params=pltpu.CompilerParams(vmem_limit_bytes=VMEM_BYTES),
        cost_estimate=pl.CostEstimate(
            flops=10 * groups * length * wide * span, bytes_accessed=16 * 2**20, transcendentals=0
        ),
    )(base, queries, block, d_mixed)


def normed_back(vector, factor, plus_gain, gradient):
    scaled = vector * factor
    inner = gradient * plus_gain
    d_vector = factor * (inner - scaled * jnp.mean(inner * scaled, axis=-1, keepdims=True))
    return d_vector, jnp.sum(gradient * scaled, axis=0, keepdims=True)


def factor_of(vector):
    return lax.rsqrt(jnp.mean(vector * vector, axis=-1, keepdims=True) + EPS)


def middle_kernel(
    sizes, x_ref, cot_ref, mixed_ref, gains_ref, *refs
):
    if sizes is None:
        out_t, gate, up, down_t = refs[:4]
        outs = refs[4:]
    else:
        first, second = refs[:2]
        outs = refs[2:12]
        out_t, gate, up, down_t = refs[12:]
    (
        y_ref, d_middle_ref, d_mixed_ref, hidden_ref, d_gate_ref, d_up_ref, ffw_in_ref,
        d_down_ref, d_attended_ref, d_gains_ref,
    ) = outs
    low = jnp.bfloat16

    @pl.when(pl.program_id(0) == 0)
    def _():
        d_gains_ref[...] = jnp.zeros_like(d_gains_ref)
        if sizes is not None:
            rows_a, rows_o, cols_f, cols_o, cols_d = sizes
            for s in range(first.shape[0]):
                for d in range(first.shape[1]):
                    tall, flat = pl.ds(s * rows_a, rows_a), pl.ds(d * rows_o, rows_o)
                    wide = pl.ds(d * cols_f, cols_f)
                    gate[tall, wide] = second[s, d, :rows_a, :cols_f]
                    up[tall, wide] = second[s, d, :rows_a, cols_f : 2 * cols_f]
                    down_t[flat, pl.ds(s * cols_d, cols_d)] = second[s, d, rows_a:, :cols_d]
                    out_t[flat, pl.ds(s * cols_o, cols_o)] = first[s, d, :, :cols_o]

    x, grad = x_ref[...].astype(jnp.float32), cot_ref[...].astype(jnp.float32)
    plus = [1.0 + gains_ref[r : r + 1, :] for r in range(4)]
    attended = dot(mixed_ref[...], out_t[...], NT)
    attended_factor = factor_of(attended)
    middle = x + attended * attended_factor * plus[1]
    middle_factor = factor_of(middle)
    ffw_in = (middle * middle_factor * plus[2]).astype(low)
    ffw_in_ref[...] = ffw_in
    a = dot(ffw_in, gate[...], NN)
    b = dot(ffw_in, up[...], NN)
    slope = math.sqrt(2.0 / math.pi)
    square = a * a
    bend = jnp.tanh(slope * a * (1.0 + 0.044715 * square))
    half = 0.5 * (1.0 + bend)
    gelu = a * half
    hidden = (gelu * b).astype(low)
    hidden_ref[...] = hidden
    down = dot(hidden, down_t[...], NT)
    down_factor = factor_of(down)
    y_ref[...] = (middle + down * down_factor * plus[3]).astype(low)
    d_down, d_out_gain = normed_back(down, down_factor, plus[3], grad)
    d_down = d_down.astype(low)
    d_down_ref[...] = d_down
    d_hidden = dot(d_down, down_t[...], NN)
    d_up = (d_hidden * gelu).astype(low)
    d_up_ref[...] = d_up
    gelu_slope = half + 0.5 * a * (1.0 - bend * bend) * (
        slope * (1.0 + 3.0 * 0.044715 * square)
    )
    d_gate = (d_hidden * b * gelu_slope).astype(low)
    d_gate_ref[...] = d_gate
    d_ffw_in = dot(d_gate, gate[...], NT) + dot(d_up, up[...], NT)
    d_middle, d_in_gain = normed_back(middle, middle_factor, plus[2], d_ffw_in)
    d_middle = grad + d_middle
    d_middle_ref[...] = d_middle
    d_attended, d_attn_gain = normed_back(attended, attended_factor, plus[1], d_middle)
    d_attended = d_attended.astype(low)
    d_attended_ref[...] = d_attended
    d_mixed_ref[...] = dot(d_attended, out_t[...], NN).astype(low)
    d_gains_ref[1:2, :] += d_attn_gain
    d_gains_ref[2:3, :] += d_in_gain
    d_gains_ref[3:4, :] += d_out_gain


def middle_part(x, cot, mixed, gains_four, weights, sizes, ff):
    tokens = x.shape[0]
    step = min(256, tokens)
    low = jnp.bfloat16
    wide = mixed.shape[1]

    def rows(cols):
        return pl.BlockSpec((step, cols), lambda i: (i, 0))

    def fixed(shape):
        return pl.BlockSpec(
            shape, lambda i: (0,) * len(shape), pipeline_mode=pl.Buffered(1)
        )

    outs = [
        (D, low), (D, jnp.float32), (wide, low), (ff, low), (ff, low), (ff, low), (D, low),
        (D, low), (D, low),
    ]
    scratch = []
    if sizes is not None:
        scratch = [pltpu.VMEM((D, cols), low) for cols in (wide, ff, ff, ff)]
    return pl.pallas_call(
        functools.partial(middle_kernel, sizes),
        grid=(tokens // step,),
        in_specs=[rows(D), rows(D), rows(wide), fixed((8, D))]
        + [fixed(weight.shape) for weight in weights],
        out_specs=[rows(cols) for cols, _ in outs] + [pl.BlockSpec((8, D), lambda i: (0, 0))],
        out_shape=[jax.ShapeDtypeStruct((tokens, cols), kind) for cols, kind in outs]
        + [jax.ShapeDtypeStruct((8, D), jnp.float32)],
        scratch_shapes=scratch,
        compiler_params=pltpu.CompilerParams(vmem_limit_bytes=VMEM_BYTES),
        cost_estimate=pl.CostEstimate(
            flops=4 * tokens * D * (3 * ff + wide), bytes_accessed=40 * 2**20, transcendentals=0
        ),
    )(x, cot, mixed, gains_four, *weights)


def out_rows(rows_o):
    return -(-rows_o // 32) * 16


def sums_kernel(
    seqs, rows_a, rows_o, cols_f, ffw_in, d_down, d_attended, d_gate, d_up, hidden, mixed, out
):
    at = pl.program_id(0)
    low = jnp.bfloat16
    each = d_gate.shape[1] // cols_f
    for half, gradient in enumerate((d_gate, d_up)):
        total = dot(ffw_in[...], gradient[...], TN).astype(low)
        for e in range(each):
            for s in range(seqs):
                out[at * each + e, s, :rows_a, half * cols_f : (half + 1) * cols_f] = total[
                    s * rows_a : (s + 1) * rows_a, e * cols_f : (e + 1) * cols_f
                ]
    total = dot(d_down[...], hidden[...], TN).astype(low)
    total_out = dot(d_attended[...], mixed[...], TN).astype(low)
    cols_o = total_out.shape[1]
    upper, last = out_rows(rows_o), rows_a + rows_o
    for d in range(out.shape[0]):
        out[d, at, rows_a:last, :] = total[d * rows_o : (d + 1) * rows_o, :]
        out[d, at, last:, :cols_o] = total_out[d * rows_o : d * rows_o + upper, :]
        out[d, at, last : last + rows_o - upper, cols_o:] = total_out[
            d * rows_o + upper : (d + 1) * rows_o, :
        ]
        if rows_o < 2 * upper:
            out[d, at, last + rows_o - upper :, cols_o:] = jnp.zeros(
                (2 * upper - rows_o, cols_o), low
            )


def packed_sums(seqs, dps, sizes, ffw_in, d_down, d_attended, d_gate, d_up, hidden, mixed):
    rows_a, rows_o, cols_f, cols_o, cols_d = sizes
    tokens = ffw_in.shape[0]
    shape = (dps, seqs, rows_a + rows_o + out_rows(rows_o), cols_d)
    whole = pl.BlockSpec((tokens, D), lambda i: (0, 0))
    part = pl.BlockSpec((tokens, cols_d), lambda i: (0, i))
    return pl.pallas_call(
        functools.partial(sums_kernel, seqs, rows_a, rows_o, cols_f),
        grid=(seqs,),
        in_specs=[whole] * 3
        + [part] * 3
        + [pl.BlockSpec((tokens, cols_o), lambda i: (0, i))],
        out_specs=pl.BlockSpec(shape, lambda i: (0, 0, 0, 0)),
        out_shape=jax.ShapeDtypeStruct(shape, jnp.bfloat16),
        compiler_params=pltpu.CompilerParams(vmem_limit_bytes=VMEM_BYTES),
        cost_estimate=pl.CostEstimate(
            flops=6 * tokens * D * cols_d * seqs, bytes_accessed=24 * 2**20, transcendentals=0
        ),
    )(ffw_in, d_down, d_attended, d_gate, d_up, hidden, mixed)


def rms_back(vector, scale_gain, gradient):
    factor = lax.rsqrt(jnp.mean(vector * vector, axis=-1, keepdims=True) + EPS)
    scaled = vector * factor
    inner = gradient * (1.0 + scale_gain)
    d_vector = factor * (inner - scaled * jnp.mean(inner * scaled, axis=-1, keepdims=True))
    d_gain = jnp.sum(gradient * scaled, axis=tuple(range(vector.ndim - 1)))
    return d_vector, d_gain


def columns_joined(gathered):
    seqs, dps, rows, cols = gathered.shape
    return gathered.transpose(0, 2, 1, 3).reshape(seqs * rows, dps * cols)


def rows_joined(gathered):
    seqs, dps, rows, cols = gathered.shape
    return gathered.transpose(1, 2, 0, 3).reshape(dps * rows, seqs * cols)


def columns_parted(whole, seqs, dps):
    rows, cols = whole.shape
    return whole.reshape(seqs, rows // seqs, dps, cols // dps).transpose(2, 0, 1, 3)


def rows_parted(whole, seqs, dps):
    rows, cols = whole.shape
    return whole.reshape(dps, rows // dps, seqs, cols // seqs).transpose(0, 2, 1, 3)


def gather(packed):
    return lax.all_gather(packed, ("seq", "dp")).reshape(
        (lax.axis_size("seq"), lax.axis_size("dp")) + packed.shape
    )


def local(inputs, cotangent, w_query, w_key, w_value, w_out, w_gate, w_up, w_down, gains):
    groups, stretch_len = inputs.shape[:2]
    seqs, dps = lax.axis_size("seq"), lax.axis_size("dp")
    heads_width = HEADS * HD
    seq_index = lax.axis_index("seq")
    query_pos = seq_index * stretch_len + jnp.arange(stretch_len, dtype=jnp.int32)
    angle_table = angles(query_pos.astype(jnp.float32), HD)
    reach = WINDOW // stretch_len
    rows_a, cols_q = w_query.shape
    cols_k = w_key.shape[1]
    rows_o = w_out.shape[1]
    rows_g, cols_g = gains.shape
    lead = cols_q + 2 * cols_k
    width = max(-(-(lead + cols_g) // 128) * 128, w_out.shape[0])

    def widened(value, rows, cols):
        return jnp.pad(value, ((0, rows - value.shape[0]), (0, cols - value.shape[1])))

    packed_one = jnp.concatenate(
        [
            widened(
                jnp.concatenate(
                    [w_query, w_key, w_value, widened(gains, rows_a, cols_g)], axis=1
                ),
                rows_a,
                width,
            ),
            widened(w_out.T, rows_o, width),
        ],
        axis=0,
    )
    cols_f = w_gate.shape[1]
    wide = max(2 * cols_f, w_down.shape[0])
    packed_two = jnp.concatenate(
        [
            widened(jnp.concatenate([w_gate, w_up], axis=1), rows_a, wide),
            widened(w_down.T, rows_o, wide),
        ],
        axis=0,
    )
    first = gather(packed_one)
    packed_two, first = lax.optimization_barrier((packed_two, first))
    second = gather(packed_two)

    full_query = columns_joined(first[:, :, :rows_a, :cols_q])
    full_key = columns_joined(first[:, :, :rows_a, cols_q : cols_q + cols_k])
    full_value = columns_joined(first[:, :, :rows_a, cols_q + cols_k : lead])
    full_gains = columns_joined(first[:, :, :rows_g, lead : lead + cols_g])
    cols_o, cols_d = w_out.shape[0], w_down.shape[0]
    sizes = (rows_a, rows_o, cols_f, cols_o, cols_d)
    aligned = (
        rows_a % 16 == 0
        and rows_o % 16 == 0
        and cols_f % 128 == 0
        and cols_o % 128 == 0
        and cols_d == 2 * cols_f
        and cols_d == 2 * cols_o
        and dps == 2 * seqs
    )
    if aligned:
        weights = (first[:, :, rows_a:, :], second)
    else:
        weights = (
            rows_joined(first[:, :, rows_a:, :cols_o]),
            columns_joined(second[:, :, :rows_a, :cols_f]),
            columns_joined(second[:, :, :rows_a, cols_f : 2 * cols_f]),
            rows_joined(second[:, :, rows_a:, :cols_d]),
        )
    g_attn_in, g_attn_out, g_ffw_in, g_ffw_out, g_query, g_key = split_gains(full_gains)

    resid = inputs.astype(jnp.float32)
    normed = rms_norm(resid, g_attn_in).astype(jnp.bfloat16)
    q_lin = product(normed, full_query).reshape(groups, stretch_len, HEADS, HD)
    k_lin = product(normed, full_key)
    v_lin = product(normed, full_value)
    keys = rotate(rms_norm(k_lin, g_key), angle_table).astype(jnp.bfloat16)
    own = jnp.concatenate([keys, v_lin.astype(jnp.bfloat16)], axis=-1)
    parts = [own]
    for offset in range(1, reach + 1):
        parts.insert(0, shifted(own, "seq", offset))
    queries = rotate(rms_norm(q_lin, g_query), angle_table[:, None, :]).astype(jnp.bfloat16)
    block = jnp.concatenate(parts, axis=1)

    base = ((seq_index - reach) * stretch_len).astype(jnp.int32).reshape(1)
    low = jnp.bfloat16
    tokens = groups * stretch_len
    queries = queries.reshape(groups, stretch_len, heads_width)
    mixed = attend(base, queries, block).reshape(tokens, heads_width)
    gains_four = jnp.pad(
        jnp.stack([g_attn_in, g_attn_out, g_ffw_in, g_ffw_out]), ((0, 4), (0, 0))
    )
    (
        outputs, d_middle, d_mixed, hidden, d_gate, d_up, ffw_in, d_down, d_attended, d_gains
    ) = middle_part(
        inputs.reshape(tokens, D),
        cotangent.reshape(tokens, D),
        mixed,
        gains_four,
        weights,
        sizes if aligned else None,
        cols_f * dps,
    )
    outputs = outputs.reshape(inputs.shape)
    d_middle = d_middle.reshape(inputs.shape)
    d_mixed = d_mixed.reshape(groups, stretch_len, heads_width)

    def widened_four(value, rows, cols):
        return jnp.pad(
            value, ((0, 0), (0, 0), (0, rows - value.shape[2]), (0, cols - value.shape[3]))
        )

    if aligned:
        early = packed_sums(
            seqs, dps, sizes, ffw_in, d_down, d_attended, d_gate, d_up, hidden, mixed
        )
    else:
        sum_gate = columns_parted(outer_sum(ffw_in, d_gate).astype(low), seqs, dps)
        sum_up = columns_parted(outer_sum(ffw_in, d_up).astype(low), seqs, dps)
        sum_down = rows_parted(outer_sum(d_down, hidden).astype(low), seqs, dps)
        sum_out = rows_parted(outer_sum(d_attended, mixed).astype(low), seqs, dps)
        upper = out_rows(rows_o)
        wide = max(wide, 2 * cols_o)
        halves = [sum_out[:, :, :upper], widened_four(sum_out[:, :, upper:], upper, cols_o)]
        early = jnp.concatenate(
            [
                widened_four(jnp.concatenate([sum_gate, sum_up], axis=3), rows_a, wide),
                widened_four(sum_down, rows_o, wide),
                widened_four(jnp.concatenate(halves, axis=3), upper, wide),
            ],
            axis=2,
        )
    early, d_mixed = lax.optimization_barrier((early, d_mixed))
    early = lax.psum_scatter(early, "dp")

    d_queries, d_block = attend_back(base, queries, block, d_mixed)
    d_queries = d_queries.reshape(groups, stretch_len, HEADS, HD)
    d_own = d_block[:, reach * stretch_len :]
    for offset in range(1, reach + 1):
        at = (reach - offset) * stretch_len
        d_own = d_own + shifted(
            d_block[:, at : at + stretch_len].astype(low), "seq", -offset
        ).astype(jnp.float32)

    def unrotate(gradient, table):
        return rotate(gradient, -table)

    d_q_lin, d_g_query = rms_back(q_lin, g_query, unrotate(d_queries, angle_table[:, None, :]))
    d_k_lin, d_g_key = rms_back(k_lin, g_key, unrotate(d_own[..., :HD], angle_table))
    d_q_lin = d_q_lin.reshape(groups, stretch_len, heads_width).astype(low)
    d_k_lin = d_k_lin.astype(low)
    d_values = d_own[..., HD:].astype(low)
    sum_query = columns_parted(outer_sum(normed, d_q_lin).astype(low), seqs, dps)
    sum_key = columns_parted(outer_sum(normed, d_k_lin).astype(low), seqs, dps)
    sum_value = columns_parted(outer_sum(normed, d_values).astype(low), seqs, dps)
    d_normed = (
        back_product(d_q_lin, full_query)
        + back_product(d_k_lin, full_key)
        + back_product(d_values, full_value)
    )
    d_resid, d_g_attn_in = rms_back(resid, g_attn_in, d_normed)
    grad_inputs = (d_middle + d_resid).astype(jnp.bfloat16)
    sum_gains = jnp.concatenate(
        [d_g_attn_in, d_gains[1], d_gains[2], d_gains[3], d_g_query, d_g_key]
    ).reshape(full_gains.shape)
    sum_gains = columns_parted(sum_gains.astype(low), seqs, dps)

    narrow = -(-(lead + cols_g) // 128) * 128
    late = widened_four(
        jnp.concatenate(
            [sum_query, sum_key, sum_value, widened_four(sum_gains, rows_a, cols_g)], axis=3
        ),
        rows_a,
        narrow,
    )
    early, late = lax.optimization_barrier((early, late))
    late = lax.psum_scatter(late, "dp")
    middle_row = rows_a // 2
    late = jnp.concatenate([late[:, :middle_row], late[:, middle_row:]], axis=2)
    early_rows = early.shape[1]
    broad = max(early.shape[2], 2 * narrow)
    both = jnp.concatenate(
        [
            jnp.pad(part, ((0, 0), (0, 0), (0, broad - part.shape[2])))
            for part in (early, late)
        ],
        axis=1,
    )
    both = lax.psum_scatter(both, "seq").astype(jnp.float32)
    early = both[:early_rows]
    late = jnp.concatenate(
        [both[early_rows:, :narrow], both[early_rows:, narrow : 2 * narrow]], axis=0
    )
    last, upper = rows_a + rows_o, out_rows(rows_o)
    grad_out = jnp.concatenate(
        [early[last:, :cols_o], early[last : last + rows_o - upper, cols_o : 2 * cols_o]], axis=0
    )
    return (
        outputs,
        grad_inputs,
        late[:rows_a, :cols_q],
        late[:rows_a, cols_q : cols_q + cols_k],
        late[:rows_a, cols_q + cols_k : lead],
        grad_out.T,
        early[:rows_a, :cols_f],
        early[:rows_a, cols_f : 2 * cols_f],
        early[rows_a:last, :cols_d].T,
        late[:rows_g, lead : lead + cols_g],
    )


def solution(mesh):
    in_specs = (
        P("dp", "seq", None),
        P("dp", "seq", None),
        P("seq", "dp"),
        P("seq", "dp"),
        P("seq", "dp"),
        P("seq", "dp"),
        P("seq", "dp"),
        P("seq", "dp"),
        P("seq", "dp"),
        P("seq", "dp"),
    )
    out_specs = (
        P("dp", "seq", None),
        P("dp", "seq", None),
        P("seq", "dp"),
        P("seq", "dp"),
        P("seq", "dp"),
        P("seq", "dp"),
        P("seq", "dp"),
        P("seq", "dp"),
        P("seq", "dp"),
        P("seq", "dp"),
    )
    return jax.shard_map(local, mesh=mesh, in_specs=in_specs, out_specs=out_specs, check_vma=False)
```
